32 devices in a mesh: chan: 16 (over z, y, core), freq: 2 (over x).
Axes of the slice: x: 2, y: 2, z: 4, core: 2. Of those that a mesh axis runs over, the one named last changes fastest.
Arguments:
- spectra: float32 [4, 2, 32, 8192], P('freq', None, 'chan'), parts along dimension 0, may hold values from -6 to 6
- alive_mask: int32 [8192], replicated, may hold values 0 or 1
Outputs:
- cross_band: float32 [16, 9, 4, 512, 1024], P('chan', None, 'freq'), parts along dimension 2
The draws below stay inside these ranges and needn't reach their ends.
There are 2 independent parts, one for each index of `freq`. The reference program is written for one: setup_inputs(seed, part) draws one part's arguments, and reference() takes and returns one part's arrays. A program takes and returns all parts, laid end to end along the dimension named above; an argument that names none is the same for every part. Nothing has to cross between parts.
All inputs are finite; a program needn't handle non-finite values.
Results may differ from the reference program's by a relative error of at most 0.0034.
Values may be sent and summed in bfloat16 or wider, within the bound.
A program may use at most 128 MiB of HBM per device.

```python
import jax
import jax.numpy as jnp
from jax import lax

C = 8192
F = 2
W = 32
LAGS = 9
N_CHAN = 16


def with_ends(result, rng, smallest, high):
    place = [jax.random.randint(jax.random.fold_in(rng, axis), (), 0, length) for axis, length in enumerate(result.shape)]
    widest = result.shape.index(max(result.shape))
    beside = place[:widest] + [(place[widest] + 1) % result.shape[widest]] + place[widest + 1:]
    return result.at[tuple(place)].set(smallest).at[tuple(beside)].set(high)


def level_of(own_key, dims, pieces, smallest, high):
    factor_of = 1.0
    for axis_at, blocks in pieces:
        draws = jax.random.uniform(jax.random.fold_in(jax.random.fold_in(own_key, 6), axis_at), (blocks,), jnp.float32, smallest / len(pieces), high / len(pieces))
        factor_of = factor_of * jnp.repeat(jnp.exp(draws), dims[axis_at] // blocks).reshape((-1,) + (1,) * (len(dims) - 1 - axis_at))
    return factor_of


def noise(own_key, shape, deviation, reach, split=(), kind=jnp.bfloat16):
    values = deviation * jax.random.normal(own_key, shape, jnp.float32)
    if split:
        values = values * level_of(own_key, shape, split, -0.22, 0.18)
    return jnp.clip(values, -reach, reach).astype(kind)


def setup_inputs(seed: int = 0, part: int = 0) -> dict:
    seeds = jax.random.split(jax.random.key(seed), 3)
    own_keys = jax.random.split(jax.random.fold_in(seeds[2], part), 3)
    return {
        "spectra": noise(own_keys[0], (F, 2, W, C), 1.0, 6.0, ((2, 16),), jnp.float32),
        "alive_mask": with_ends((jax.random.randint(seeds[1], (C,), 0, 16) < 15).astype(jnp.int32), jax.random.fold_in(seeds[1], 1), 0, 1),
    }


def whiten(spectra, alive_mask):
    real_part = spectra[:, 0]
    imag_part = spectra[:, 1]
    magnitude = jnp.sqrt(real_part * real_part + imag_part * imag_part)
    factor = alive_mask.astype(jnp.float32)[None, None, :] / jnp.maximum(magnitude, 1.0)
    return (spectra * factor[:, None]).astype(jnp.bfloat16)

def stack_own(own_block):
    middle = own_block.shape[1] // 2
    turned = jnp.concatenate([own_block[:, middle:], -own_block[:, :middle]], axis=1)
    return jnp.concatenate([own_block, turned], axis=2)

def cross_block(own_stacked, partner_block, windows):
    product = jnp.einsum('fwj,fwi->fji', partner_block.astype(jnp.float32), own_stacked.astype(jnp.float32), precision=lax.Precision.HIGHEST)
    return product / windows

def reference(spectra, alive_mask):
    whitened = whiten(spectra, alive_mask)
    blocks = whitened.reshape(F, 2 * W, N_CHAN, C // N_CHAN).transpose(2, 0, 1, 3)
    lag_range = jnp.arange(LAGS, dtype=jnp.int32)

    def one_row(row_index):
        own_stacked = stack_own(blocks[row_index])
        partners = blocks[(row_index - lag_range) % N_CHAN]

        def with_partner(partner_block):
            return cross_block(own_stacked, partner_block, W)
        return lax.map(with_partner, partners)
    return lax.map(one_row, jnp.arange(N_CHAN, dtype=jnp.int32))
```

```python
import functools

import jax
import jax.numpy as jnp
from jax import lax
from jax.experimental import pallas as pl
from jax.experimental.pallas import tpu as pltpu
from jax.sharding import PartitionSpec as P

MESH = pl.DeviceIdType.MESH
PLANES = 4
SLOTS = 16

UP = {0: [(0, 4), (4, 4), (8, 4)], 1: [(0, 4), (4, 4)], 2: [(2, 2), (4, 4)]}
DOWN = {3: [(4, 4), (8, 4), (0, 4)], 2: [(4, 4), (8, 4)], 1: [(4, 4), (8, 2)]}


def from_behind(block, axis, distance):
    devices = range(lax.axis_size(axis))
    route = [((i - distance) % len(devices), i) for i in devices]
    return lax.ppermute(block, axis, route)


def cross_block(own_stacked, partner_block, windows):
    product = jnp.einsum(
        "fjw,fiw->fji", partner_block, own_stacked, preferred_element_type=jnp.float32
    )
    return product / windows


def ring_shards(spectra, alive_mask):
    channel_devices = lax.axis_size("chan")
    groups = spectra.shape[0]
    block_width = spectra.shape[3] // channel_devices
    windows = spectra.shape[2] * channel_devices
    lag_count = channel_devices // 2 + 1
    real_part = spectra[:, 0]
    imag_part = spectra[:, 1]
    magnitude = jnp.sqrt(real_part * real_part + imag_part * imag_part)
    factor = alive_mask.astype(jnp.float32)[None, None, :] / jnp.maximum(magnitude, 1.0)
    whitened = (spectra * factor[:, None]).astype(jnp.bfloat16)
    regrouped = lax.all_to_all(whitened, "chan", split_axis=3, concat_axis=2, tiled=True)
    own_block = jnp.transpose(regrouped.reshape(groups, 2 * windows, block_width), (0, 2, 1))
    turned = jnp.concatenate([own_block[:, :, windows:], -own_block[:, :, :windows]], axis=2)
    own_stacked = jnp.concatenate([own_block, turned], axis=1)
    empty_band = jnp.zeros((lag_count, groups, block_width, 2 * block_width), jnp.float32)
    start_band = lax.dynamic_update_index_in_dim(
        empty_band, cross_block(own_stacked, own_block, windows), 0, 0
    )

    def four_steps(turn, carry):
        visitor, band = carry
        for repeat in range(4):
            visitor = from_behind(visitor, "chan", 1)
            band = lax.dynamic_update_index_in_dim(
                band, cross_block(own_stacked, visitor, windows), 1 + 4 * turn + repeat, 0
            )
        return (visitor, band)

    visitor, cross_band = lax.fori_loop(
        0, channel_devices // 8, four_steps, (own_block, start_band)
    )
    return cross_band[None]


def gather_kernel(x_hbm, alive_ref, h_ref, x_buf, g, load_sem, recv_z, recv_y, recv_c, send_z, send_y, send_c, out_sem):
    me = lax.axis_index("chan")
    z, y, c = me // 4, (me // 2) % 2, me % 2
    y_peer = z * 4 + (1 - y) * 2 + c
    c_peer = z * 4 + y * 2 + (1 - c)
    width = x_buf.shape[1] // 16

    loads = []
    for f in range(2):
        for part in range(2):
            at = f * 2 + part
            loads.append(pltpu.make_async_copy(x_hbm.at[f, part], x_buf.at[pl.ds(2 * at, 2)], load_sem.at[at]))
    for load in loads:
        load.start()

    barrier = pltpu.get_barrier_semaphore()
    pl.semaphore_signal(barrier, inc=1, device_id={"chan": y_peer}, device_id_type=MESH)
    pl.semaphore_signal(barrier, inc=1, device_id={"chan": c_peer}, device_id_type=MESH)

    @pl.when(z < PLANES - 1)
    def _():
        pl.semaphore_signal(barrier, inc=1, device_id={"chan": me + 4}, device_id_type=MESH)

    @pl.when(z > 0)
    def _():
        pl.semaphore_signal(barrier, inc=1, device_id={"chan": me - 4}, device_id_type=MESH)

    for load in loads:
        load.wait()
    for granule in range(8):
        halves = []
        for half in range(2):
            at = pl.ds((2 * granule + half) * width, width)
            x = x_buf[:, at]
            square = x * x
            row = lax.broadcasted_iota(jnp.int32, x.shape, 0)
            is_real = (row // 2) % 2 == 0
            other = jnp.where(is_real, pltpu.roll(square, 6, 0), pltpu.roll(square, 2, 0))
            magnitude = jnp.sqrt(square + other)
            factor = alive_ref[:, at].astype(jnp.float32) / jnp.maximum(magnitude, 1.0)
            halves.append(x * factor)
        tile = jnp.concatenate(halves, axis=0).astype(jnp.bfloat16)
        g[me, granule] = tile
        g[me, granule + 8] = tile

    @pl.when((z == 0) | (z == PLANES - 1))
    def _():
        pl.semaphore_wait(barrier, 3)

    @pl.when((z > 0) & (z < PLANES - 1))
    def _():
        pl.semaphore_wait(barrier, 4)

    def remote(src, start, length, peer, send, recv):
        view = g.at[src, pl.ds(start, length)]
        return pltpu.make_async_remote_copy(
            src_ref=view, dst_ref=view, send_sem=send, recv_sem=recv,
            device_id={"chan": peer}, device_id_type=MESH,
        )

    def plane(zz):
        base = (2 * zz + 4) % 8
        column = lambda s: s * 4 + y * 2 + c
        others = lambda s: s * 4 + (1 - y) * 2 + c
        mine = base + y
        sends = []
        outs = []

        def go(copy):
            copy.start()
            sends.append(copy)

        def up(s, k):
            start, length = UP[zz][k]
            go(remote(column(s), start, length, me + 4, send_z.at[0, s, k], recv_z.at[s, k]))

        def down(s, k):
            start, length = DOWN[zz][k]
            go(remote(column(s), start, length, me - 4, send_z.at[1, s, k], recv_z.at[s, k]))

        def to_y(s):
            go(remote(column(s), base + (1 - y), 5, y_peer, send_y.at[s], recv_y.at[s]))

        def to_c(src, at):
            go(remote(src, mine, 5, c_peer, send_c.at[at], recv_c.at[at]))

        def keep(src, at):
            copy = pltpu.make_async_copy(g.at[src, pl.ds(mine, 5)], h_ref.at[:, src], out_sem.at[at])
            copy.start()
            outs.append(copy)

        def from_z(s):
            windows = UP[zz - 1] if s < zz else DOWN[zz + 1]
            for k, (start, length) in enumerate(windows):
                remote(column(s), start, length, me, send_z.at[0, s, k], recv_z.at[s, k]).wait_recv()
                if s < zz and zz < PLANES - 1 and k < len(UP[zz]):
                    up(s, k)
                if s > zz and zz > 0 and k < len(DOWN[zz]):
                    down(s, k)
            to_y(s)
            to_c(column(s), s)
            keep(column(s), s)

        def from_y(s):
            remote(others(s), mine, 5, me, send_y.at[s], recv_y.at[s]).wait_recv()
            to_c(others(s), 4 + s)
            keep(others(s), 4 + s)

        def from_c(s, in_column):
            src = s * 4 + (y if in_column else 1 - y) * 2 + (1 - c)
            at = s if in_column else 4 + s
            remote(src, mine, 5, me, send_c.at[at], recv_c.at[at]).wait_recv()
            keep(src, 8 + at)

        order = sorted((s for s in range(PLANES) if s != zz), key=lambda s: abs(s - zz))
        for k in range(3):
            if zz < PLANES - 1 and k < len(UP[zz]):
                up(zz, k)
            if zz > 0 and k < len(DOWN[zz]):
                down(zz, k)
        to_y(zz)
        to_c(me, zz)
        keep(me, zz)
        from_z(order[0])
        from_y(zz)
        from_z(order[1])
        from_y(order[0])
        from_z(order[2])
        from_y(order[1])
        from_y(order[2])
        from_c(zz, True)
        from_c(order[0], True)
        from_c(zz, False)
        from_c(order[1], True)
        from_c(order[0], False)
        from_c(order[2], True)
        from_c(order[1], False)
        from_c(order[2], False)
        for copy in sends:
            copy.wait_send()
        for copy in outs:
            copy.wait()

    for zz in range(PLANES):
        pl.when(z == zz)(functools.partial(plane, zz))


def gather(spectra, alive_mask):
    width = spectra.shape[3] // 16
    return pl.pallas_call(
        gather_kernel,
        out_shape=jax.ShapeDtypeStruct((5, 16, 16, width), jnp.bfloat16),
        in_specs=[pl.BlockSpec(memory_space=pl.ANY), pl.BlockSpec(memory_space=pltpu.VMEM)],
        out_specs=pl.BlockSpec(memory_space=pl.ANY),
        scratch_shapes=[
            pltpu.VMEM((8, 16 * width), jnp.float32),
            pltpu.VMEM((16, SLOTS, 16, width), jnp.bfloat16),
            pltpu.SemaphoreType.DMA((4,)),
            pltpu.SemaphoreType.DMA((4, 3)),
            pltpu.SemaphoreType.DMA((4,)),
            pltpu.SemaphoreType.DMA((8,)),
            pltpu.SemaphoreType.DMA((2, 4, 3)),
            pltpu.SemaphoreType.DMA((4,)),
            pltpu.SemaphoreType.DMA((8,)),
            pltpu.SemaphoreType.DMA((16,)),
        ],
        compiler_params=pltpu.CompilerParams(
            collective_id=0, has_side_effects=True, vmem_limit_bytes=24 * 2**20
        ),
        name="gather",
    )(spectra, alive_mask.reshape(1, -1))


def cross_kernel(scale, h_ref, out_ref, own, turned_rows):
    step = pl.program_id(0)
    c = lax.axis_index("chan") % 2
    rows = h_ref.shape[1] * h_ref.shape[2]
    width = h_ref.shape[3]

    @pl.when(step == 0)
    def _():
        x = h_ref[4].reshape(rows, width).astype(jnp.float32)
        row = lax.broadcasted_iota(jnp.int32, x.shape, 0)
        block, group, part = (row // 8) % 2, (row // 4) % 2, (row // 2) % 2
        swapped = jnp.where(block == 0, pltpu.roll(x, rows - 8, 0), pltpu.roll(x, 8, 0))
        for t in range(2):
            base = jnp.where(c == t, x, swapped)
            turned = jnp.where(part == 0, pltpu.roll(base, rows - 2, 0), -pltpu.roll(base, 2, 0))
            for f in range(2):
                kept = (block == t) & (group == f)
                own[t, f, :, pl.ds(0, width)] = jnp.where(kept, base, 0.0).astype(jnp.bfloat16)
                own[t, f, :, pl.ds(width, width)] = jnp.where(kept, turned, 0.0).astype(jnp.bfloat16)
        for q in range(5):
            turned_rows[q] = h_ref[q].reshape(rows, width).T

    place = 8 + c - step // 2
    product = jnp.dot(
        turned_rows[place // 2], own[place % 2, step % 2], preferred_element_type=jnp.float32
    )
    out_ref[0, 0] = product * scale


def cross(gathered, windows):
    width = gathered.shape[3]
    return pl.pallas_call(
        functools.partial(cross_kernel, 1.0 / windows),
        out_shape=jax.ShapeDtypeStruct((9, 2, width, 2 * width), jnp.float32),
        grid=(18,),
        in_specs=[pl.BlockSpec(memory_space=pltpu.VMEM)],
        out_specs=pl.BlockSpec((1, 1, width, 2 * width), lambda i: (i // 2, i % 2, 0, 0)),
        scratch_shapes=[
            pltpu.VMEM((2, 2, 256, 2 * width), jnp.bfloat16),
            pltpu.VMEM((5, width, 256), jnp.bfloat16),
        ],
        compiler_params=pltpu.CompilerParams(vmem_limit_bytes=40 * 2**20),
        name="cross",
    )(gathered)


def plane_shards(spectra, alive_mask):
    gathered = gather(spectra, alive_mask)
    return cross(gathered, 16 * spectra.shape[2])[None]


def solution(mesh):
    def local(spectra, alive_mask):
        fits = lax.axis_size("chan") == 16 and spectra.shape == (2, 2, 2, 8192)
        return (plane_shards if fits else ring_shards)(spectra, alive_mask)

    return jax.shard_map(
        local,
        mesh=mesh,
        in_specs=(P("freq", None, "chan", None), P()),
        out_specs=P("chan", None, "freq", None, None),
        check_vma=False,
    )
```

```python
import functools

import jax
import jax.numpy as jnp
from jax import lax
from jax.experimental import pallas as pl
from jax.experimental.pallas import tpu as pltpu
from jax.sharding import PartitionSpec as P

MESH = pl.DeviceIdType.MESH
PLANES = 4
SLOTS = 16
LAGS = 9
DEPTH = 4
HALVES = 2

UP = {0: [(0, 4), (4, 4), (8, 4)], 1: [(0, 4), (4, 4)], 2: [(2, 2), (4, 4)]}
DOWN = {3: [(4, 4), (8, 4), (0, 4)], 2: [(4, 4), (8, 4)], 1: [(4, 4), (8, 2)]}


def from_behind(block, axis, distance):
    devices = range(lax.axis_size(axis))
    route = [((i - distance) % len(devices), i) for i in devices]
    return lax.ppermute(block, axis, route)


def cross_block(own_stacked, partner_block, windows):
    product = jnp.einsum(
        "fjw,fiw->fji", partner_block, own_stacked, preferred_element_type=jnp.float32
    )
    return product / windows


def ring_shards(spectra, alive_mask):
    channel_devices = lax.axis_size("chan")
    groups = spectra.shape[0]
    block_width = spectra.shape[3] // channel_devices
    windows = spectra.shape[2] * channel_devices
    lag_count = channel_devices // 2 + 1
    real_part = spectra[:, 0]
    imag_part = spectra[:, 1]
    magnitude = jnp.sqrt(real_part * real_part + imag_part * imag_part)
    factor = alive_mask.astype(jnp.float32)[None, None, :] / jnp.maximum(magnitude, 1.0)
    whitened = (spectra * factor[:, None]).astype(jnp.bfloat16)
    regrouped = lax.all_to_all(whitened, "chan", split_axis=3, concat_axis=2, tiled=True)
    own_block = jnp.transpose(regrouped.reshape(groups, 2 * windows, block_width), (0, 2, 1))
    turned = jnp.concatenate([own_block[:, :, windows:], -own_block[:, :, :windows]], axis=2)
    own_stacked = jnp.concatenate([own_block, turned], axis=1)
    empty_band = jnp.zeros((lag_count, groups, block_width, 2 * block_width), jnp.float32)
    start_band = lax.dynamic_update_index_in_dim(
        empty_band, cross_block(own_stacked, own_block, windows), 0, 0
    )

    def four_steps(turn, carry):
        visitor, band = carry
        for repeat in range(4):
            visitor = from_behind(visitor, "chan", 1)
            band = lax.dynamic_update_index_in_dim(
                band, cross_block(own_stacked, visitor, windows), 1 + 4 * turn + repeat, 0
            )
        return (visitor, band)

    visitor, cross_band = lax.fori_loop(
        0, channel_devices // 8, four_steps, (own_block, start_band)
    )
    return cross_band[None]


def gather_kernel(x_hbm, alive_hbm, h_ref, x_buf, alive_ref, g, load_sem, recv_z, recv_y, recv_c, send_z, send_y, send_c, out_sem):
    me = lax.axis_index("chan")
    z, y, c = me // 4, (me // 2) % 2, me % 2
    y_peer = z * 4 + (1 - y) * 2 + c
    c_peer = z * 4 + y * 2 + (1 - c)
    width = x_buf.shape[1] // 16

    loads = []
    for f in range(2):
        for part in range(2):
            at = f * 2 + part
            loads.append(pltpu.make_async_copy(x_hbm.at[f, part], x_buf.at[pl.ds(2 * at, 2)], load_sem.at[at]))
    loads.append(pltpu.make_async_copy(alive_hbm, alive_ref, load_sem.at[4]))
    for load in loads:
        load.start()

    barrier = pltpu.get_barrier_semaphore()
    pl.semaphore_signal(barrier, inc=1, device_id={"chan": y_peer}, device_id_type=MESH)
    pl.semaphore_signal(barrier, inc=1, device_id={"chan": c_peer}, device_id_type=MESH)

    @pl.when(z < PLANES - 1)
    def _():
        pl.semaphore_signal(barrier, inc=1, device_id={"chan": me + 4}, device_id_type=MESH)

    @pl.when(z > 0)
    def _():
        pl.semaphore_signal(barrier, inc=1, device_id={"chan": me - 4}, device_id_type=MESH)

    for load in loads:
        load.wait()
    for granule in range(8):
        halves = []
        for half in range(2):
            at = pl.ds((2 * granule + half) * width, width)
            x = x_buf[:, at]
            square = x * x
            row = lax.broadcasted_iota(jnp.int32, x.shape, 0)
            is_real = (row // 2) % 2 == 0
            other = jnp.where(is_real, pltpu.roll(square, 6, 0), pltpu.roll(square, 2, 0))
            magnitude = jnp.sqrt(square + other)
            factor = alive_ref[:, at].astype(jnp.float32) / jnp.maximum(magnitude, 1.0)
            halves.append(x * factor)
        tile = jnp.concatenate(halves, axis=0).astype(jnp.bfloat16)
        g[me, granule] = tile
        g[me, granule + 8] = tile

    @pl.when((z == 0) | (z == PLANES - 1))
    def _():
        pl.semaphore_wait(barrier, 3)

    @pl.when((z > 0) & (z < PLANES - 1))
    def _():
        pl.semaphore_wait(barrier, 4)

    def remote(src, start, length, peer, send, recv):
        view = g.at[src, pl.ds(start, length)]
        return pltpu.make_async_remote_copy(
            src_ref=view, dst_ref=view, send_sem=send, recv_sem=recv,
            device_id={"chan": peer}, device_id_type=MESH,
        )

    def plane(zz):
        base = (2 * zz + 4) % 8
        column = lambda s: s * 4 + y * 2 + c
        others = lambda s: s * 4 + (1 - y) * 2 + c
        mine = base + y
        sends = []
        outs = []

        def go(copy):
            copy.start()
            sends.append(copy)

        def up(s, k):
            start, length = UP[zz][k]
            go(remote(column(s), start, length, me + 4, send_z.at[0, s, k], recv_z.at[s, k]))

        def down(s, k):
            start, length = DOWN[zz][k]
            go(remote(column(s), start, length, me - 4, send_z.at[1, s, k], recv_z.at[s, k]))

        def to_y(s):
            go(remote(column(s), base + (1 - y), 5, y_peer, send_y.at[s], recv_y.at[s]))

        def to_c(src, at):
            go(remote(src, mine, 5, c_peer, send_c.at[at], recv_c.at[at]))

        def keep(src, at):
            copy = pltpu.make_async_copy(g.at[src, pl.ds(mine, 5)], h_ref.at[:, src], out_sem.at[at])
            copy.start()
            outs.append(copy)

        def from_z(s):
            windows = UP[zz - 1] if s < zz else DOWN[zz + 1]
            for k, (start, length) in enumerate(windows):
                remote(column(s), start, length, me, send_z.at[0, s, k], recv_z.at[s, k]).wait_recv()
                if s < zz and zz < PLANES - 1 and k < len(UP[zz]):
                    up(s, k)
                if s > zz and zz > 0 and k < len(DOWN[zz]):
                    down(s, k)
            to_y(s)
            to_c(column(s), s)
            keep(column(s), s)

        def from_y(s):
            remote(others(s), mine, 5, me, send_y.at[s], recv_y.at[s]).wait_recv()
            to_c(others(s), 4 + s)
            keep(others(s), 4 + s)

        def from_c(s, in_column):
            src = s * 4 + (y if in_column else 1 - y) * 2 + (1 - c)
            at = s if in_column else 4 + s
            remote(src, mine, 5, me, send_c.at[at], recv_c.at[at]).wait_recv()
            keep(src, 8 + at)

        order = sorted((s for s in range(PLANES) if s != zz), key=lambda s: abs(s - zz))
        for k in range(3):
            if zz < PLANES - 1 and k < len(UP[zz]):
                up(zz, k)
            if zz > 0 and k < len(DOWN[zz]):
                down(zz, k)
        to_y(zz)
        to_c(me, zz)
        keep(me, zz)
        from_z(order[0])
        from_y(zz)
        from_z(order[1])
        from_y(order[0])
        from_z(order[2])
        from_y(order[1])
        from_y(order[2])
        from_c(zz, True)
        from_c(order[0], True)
        from_c(zz, False)
        from_c(order[1], True)
        from_c(order[0], False)
        from_c(order[2], True)
        from_c(order[1], False)
        from_c(order[2], False)
        for copy in sends:
            copy.wait_send()
        for copy in outs:
            copy.wait()

    for zz in range(PLANES):
        pl.when(z == zz)(functools.partial(plane, zz))


def gather(spectra, alive_mask):
    width = spectra.shape[3] // 16
    return pl.pallas_call(
        gather_kernel,
        out_shape=jax.ShapeDtypeStruct((5, 16, 16, width), jnp.bfloat16),
        in_specs=[pl.BlockSpec(memory_space=pltpu.HBM)] * 2,
        out_specs=pl.BlockSpec(memory_space=pl.ANY),
        scratch_shapes=[
            pltpu.VMEM((8, 16 * width), jnp.float32),
            pltpu.VMEM((1, 16 * width), jnp.int32),
            pltpu.VMEM((16, SLOTS, 16, width), jnp.bfloat16),
            pltpu.SemaphoreType.DMA((5,)),
            pltpu.SemaphoreType.DMA((4, 3)),
            pltpu.SemaphoreType.DMA((4,)),
            pltpu.SemaphoreType.DMA((8,)),
            pltpu.SemaphoreType.DMA((2, 4, 3)),
            pltpu.SemaphoreType.DMA((4,)),
            pltpu.SemaphoreType.DMA((8,)),
            pltpu.SemaphoreType.DMA((16,)),
        ],
        compiler_params=pltpu.CompilerParams(
            collective_id=0, has_side_effects=True, vmem_limit_bytes=24 * 2**20
        ),
        name="gather",
    )(
        pltpu.with_memory_space_constraint(spectra, pltpu.HBM),
        pltpu.with_memory_space_constraint(alive_mask.reshape(1, -1), pltpu.HBM),
    )


def cross_kernel(scale, h_ref, out_ref, own, partner, ring, sems):
    c = lax.axis_index("chan") % 2
    rows = h_ref.shape[1] * h_ref.shape[2]
    width = h_ref.shape[3]
    half = width // HALVES

    def out_copy(lag, f, piece):
        slot = lag % DEPTH
        return pltpu.make_async_copy(
            ring.at[slot, f, pl.ds(piece * half, half)],
            out_ref.at[lag, f, pl.ds(piece * half, half)],
            sems.at[slot, f, piece],
        )

    def one_lag(lag, _):
        place = 8 + c - lag
        kind = place % 2

        @pl.when(lag < 2)
        def _():
            x = h_ref[4].reshape(rows, width).astype(jnp.float32)
            row = lax.broadcasted_iota(jnp.int32, x.shape, 0)
            block, group, part = (row // 8) % 2, (row // 4) % 2, (row // 2) % 2
            swapped = jnp.where(block == 0, pltpu.roll(x, rows - 8, 0), pltpu.roll(x, 8, 0))
            base = jnp.where(lag == 0, x, swapped)
            turned = jnp.where(part == 0, pltpu.roll(base, rows - 2, 0), -pltpu.roll(base, 2, 0))
            for f in range(2):
                kept = (block == kind) & (group == f)
                own[kind, f, :, pl.ds(0, width)] = jnp.where(kept, base, 0.0).astype(jnp.bfloat16)
                own[kind, f, :, pl.ds(width, width)] = jnp.where(kept, turned, 0.0).astype(jnp.bfloat16)

        @pl.when((lag == 0) | (kind == 1))
        def _():
            partner[...] = h_ref[place // 2].reshape(rows, width).T

        for f in range(2):
            for piece in range(HALVES):
                at = pl.ds(piece * half, half)
                product = jnp.dot(partner[at, :], own[kind, f], preferred_element_type=jnp.float32)

                @pl.when(lag >= DEPTH)
                def _():
                    out_copy(lag - DEPTH, f, piece).wait()

                ring[lag % DEPTH, f, at] = product * scale
                out_copy(lag, f, piece).start()
        return 0

    lax.fori_loop(0, LAGS, one_lag, 0)
    for lag in range(LAGS - DEPTH, LAGS):
        for f in range(2):
            for piece in range(HALVES):
                out_copy(lag, f, piece).wait()


def cross(gathered, windows):
    width = gathered.shape[3]
    return pl.pallas_call(
        functools.partial(cross_kernel, 1.0 / windows),
        out_shape=jax.ShapeDtypeStruct((LAGS, 2, width, 2 * width), jnp.float32),
        in_specs=[pl.BlockSpec(memory_space=pltpu.VMEM)],
        out_specs=pl.BlockSpec(memory_space=pltpu.HBM),
        scratch_shapes=[
            pltpu.VMEM((2, 2, 256, 2 * width), jnp.bfloat16),
            pltpu.VMEM((width, 256), jnp.bfloat16),
            pltpu.VMEM((DEPTH, 2, width, 2 * width), jnp.float32),
            pltpu.SemaphoreType.DMA((DEPTH, 2, HALVES)),
        ],
        compiler_params=pltpu.CompilerParams(vmem_limit_bytes=28 * 2**20),
        name="cross",
    )(gathered)


def plane_shards(spectra, alive_mask):
    gathered = gather(spectra, alive_mask)
    return cross(gathered, 16 * spectra.shape[2])[None]


def solution(mesh):
    def local(spectra, alive_mask):
        fits = lax.axis_size("chan") == 16 and spectra.shape == (2, 2, 2, 8192)
        return (plane_shards if fits else ring_shards)(spectra, alive_mask)

    return jax.shard_map(
        local,
        mesh=mesh,
        in_specs=(P("freq", None, "chan", None), P()),
        out_specs=P("chan", None, "freq", None, None),
        check_vma=False,
    )
```

```python
import functools

import jax
import jax.numpy as jnp
from jax import lax
from jax.experimental import pallas as pl
from jax.experimental.pallas import tpu as pltpu
from jax.sharding import PartitionSpec as P

MESH = pl.DeviceIdType.MESH
PLANES = 4
SLOTS = 16
LAGS = 9
DEPTH = 4
HALVES = 2

PIECES = [(0, 3), (3, 3)]
NEED = 6


def from_behind(block, axis, distance):
    devices = range(lax.axis_size(axis))
    route = [((i - distance) % len(devices), i) for i in devices]
    return lax.ppermute(block, axis, route)


def cross_block(own_stacked, partner_block, windows):
    product = jnp.einsum(
        "fjw,fiw->fji", partner_block, own_stacked, preferred_element_type=jnp.float32
    )
    return product / windows


def ring_shards(spectra, alive_mask):
    channel_devices = lax.axis_size("chan")
    groups = spectra.shape[0]
    block_width = spectra.shape[3] // channel_devices
    windows = spectra.shape[2] * channel_devices
    lag_count = channel_devices // 2 + 1
    real_part = spectra[:, 0]
    imag_part = spectra[:, 1]
    magnitude = jnp.sqrt(real_part * real_part + imag_part * imag_part)
    factor = alive_mask.astype(jnp.float32)[None, None, :] / jnp.maximum(magnitude, 1.0)
    whitened = (spectra * factor[:, None]).astype(jnp.bfloat16)
    regrouped = lax.all_to_all(whitened, "chan", split_axis=3, concat_axis=2, tiled=True)
    own_block = jnp.transpose(regrouped.reshape(groups, 2 * windows, block_width), (0, 2, 1))
    turned = jnp.concatenate([own_block[:, :, windows:], -own_block[:, :, :windows]], axis=2)
    own_stacked = jnp.concatenate([own_block, turned], axis=1)
    empty_band = jnp.zeros((lag_count, groups, block_width, 2 * block_width), jnp.float32)
    start_band = lax.dynamic_update_index_in_dim(
        empty_band, cross_block(own_stacked, own_block, windows), 0, 0
    )

    def four_steps(turn, carry):
        visitor, band = carry
        for repeat in range(4):
            visitor = from_behind(visitor, "chan", 1)
            band = lax.dynamic_update_index_in_dim(
                band, cross_block(own_stacked, visitor, windows), 1 + 4 * turn + repeat, 0
            )
        return (visitor, band)

    visitor, cross_band = lax.fori_loop(
        0, channel_devices // 8, four_steps, (own_block, start_band)
    )
    return cross_band[None]


def gather_kernel(x_hbm, alive_hbm, h_ref, x_buf, alive_ref, g, load_sem, recv_z, recv_y, recv_c, send_z, send_y, send_c, out_sem):
    me = lax.axis_index("chan")
    z, y, c = me // 4, (me // 2) % 2, me % 2
    y_peer = z * 4 + (1 - y) * 2 + c
    c_peer = z * 4 + y * 2 + (1 - c)
    width = x_buf.shape[1] // 16

    loads = []
    for f in range(2):
        for part in range(2):
            at = f * 2 + part
            loads.append(pltpu.make_async_copy(x_hbm.at[f, part], x_buf.at[pl.ds(2 * at, 2)], load_sem.at[at]))
    loads.append(pltpu.make_async_copy(alive_hbm, alive_ref, load_sem.at[4]))
    for load in loads:
        load.start()

    barrier = pltpu.get_barrier_semaphore()
    pl.semaphore_signal(barrier, inc=1, device_id={"chan": y_peer}, device_id_type=MESH)
    pl.semaphore_signal(barrier, inc=1, device_id={"chan": c_peer}, device_id_type=MESH)

    for hop in range(1, PLANES):
        pl.semaphore_signal(barrier, inc=1, device_id={"chan": (me + 4 * hop) % 16}, device_id_type=MESH)

    for load in loads:
        load.wait()
    for granule in range(8):
        halves = []
        for half in range(2):
            at = pl.ds((2 * granule + half) * width, width)
            x = x_buf[:, at]
            square = x * x
            row = lax.broadcasted_iota(jnp.int32, x.shape, 0)
            is_real = (row // 2) % 2 == 0
            other = jnp.where(is_real, pltpu.roll(square, 6, 0), pltpu.roll(square, 2, 0))
            magnitude = jnp.sqrt(square + other)
            factor = alive_ref[:, at].astype(jnp.float32) / jnp.maximum(magnitude, 1.0)
            halves.append(x * factor)
        tile = jnp.concatenate(halves, axis=0).astype(jnp.bfloat16)
        g[granule] = tile
        g[granule + 8] = tile

    pl.semaphore_wait(barrier, 5)

    def chip(zz, yy):
        first = lambda plane: (2 * plane + 4) % 8
        column = lambda s: s * 4 + yy * 2 + c
        others = lambda s: s * 4 + (1 - yy) * 2 + c
        sends = []

        def remote(view, src, start, length, peer, send, recv):
            return pltpu.make_async_remote_copy(
                src_ref=view, dst_ref=h_ref.at[pl.ds(start, length), src], send_sem=send, recv_sem=recv,
                device_id={"chan": peer}, device_id_type=MESH,
            )

        def go(copy):
            copy.start()
            sends.append(copy)

        def cut(k, chip_y):
            start, length = PIECES[k]
            low, high = max(start, chip_y), min(start + length, chip_y + 5)
            return low, high - low

        def view_of(s, start, length):
            if s == zz:
                return g.at[pl.ds(first(zz) + start, length)]
            return h_ref.at[pl.ds(start, length), column(s)]

        def to_z(s, k):
            start, length = PIECES[k]
            view = g.at[pl.ds(first(s) + start, length)]
            go(remote(view, me, start, length, s * 4 + yy * 2 + c, send_z.at[s, k], recv_z.at[zz, k]))

        def to_y(s, k):
            start, length = cut(k, 1 - yy)
            go(remote(view_of(s, start, length), column(s), start, length, y_peer, send_y.at[s, k], recv_y.at[s, k]))

        def to_c(s, k, in_column):
            start, length = cut(k, yy)
            src = column(s) if in_column else others(s)
            view = view_of(s, start, length) if in_column else h_ref.at[pl.ds(start, length), src]
            at = s if in_column else PLANES + s
            go(remote(view, src, start, length, c_peer, send_c.at[at, k], recv_c.at[at, k]))

        def from_z(s, k):
            start, length = PIECES[k]
            view = g.at[pl.ds(start, length)]
            remote(view, column(s), start, length, y_peer, send_z.at[s, k], recv_z.at[s, k]).wait_recv()
            to_y(s, k)
            to_c(s, k, True)

        def from_y(s, k):
            start, length = cut(k, yy)
            view = g.at[pl.ds(start, length)]
            remote(view, others(s), start, length, y_peer, send_y.at[s, k], recv_y.at[s, k]).wait_recv()
            to_c(s, k, False)

        def from_c(s, k, in_column):
            start, length = cut(k, yy)
            src = s * 4 + (yy if in_column else 1 - yy) * 2 + (1 - c)
            at = s if in_column else PLANES + s
            view = g.at[pl.ds(start, length)]
            remote(view, src, start, length, c_peer, send_c.at[at, k], recv_c.at[at, k]).wait_recv()

        order = sorted((s for s in range(PLANES) if s != zz), key=lambda s: abs(s - zz))
        count = len(PIECES)
        for k in range(count):
            for s in reversed(order):
                to_z(s, k)
            to_y(zz, k)
        for k in range(count):
            to_c(zz, k, True)
        keep = pltpu.make_async_copy(g.at[pl.ds(first(zz), NEED)], h_ref.at[:, me], out_sem)
        keep.start()
        for k in range(count):
            from_y(zz, k)
            for s in order:
                from_z(s, k)
                if k > 0:
                    from_y(s, k - 1)
        for s in order:
            from_y(s, count - 1)
        for k in range(count):
            for in_column in (True, False):
                for s in [zz] + order:
                    from_c(s, k, in_column)
        for copy in sends:
            copy.wait_send()
        keep.wait()

    for zz in range(PLANES):
        for yy in range(2):
            pl.when((z == zz) & (y == yy))(functools.partial(chip, zz, yy))


def gather(spectra, alive_mask):
    width = spectra.shape[3] // 16
    return pl.pallas_call(
        gather_kernel,
        out_shape=jax.ShapeDtypeStruct((NEED, 16, 16, width), jnp.bfloat16),
        in_specs=[pl.BlockSpec(memory_space=pltpu.HBM)] * 2,
        out_specs=pl.BlockSpec(memory_space=pl.ANY),
        scratch_shapes=[
            pltpu.VMEM((8, 16 * width), jnp.float32),
            pltpu.VMEM((1, 16 * width), jnp.int32),
            pltpu.VMEM((SLOTS, 16, width), jnp.bfloat16),
            pltpu.SemaphoreType.DMA((5,)),
            pltpu.SemaphoreType.DMA((4, len(PIECES))),
            pltpu.SemaphoreType.DMA((4, len(PIECES))),
            pltpu.SemaphoreType.DMA((8, len(PIECES))),
            pltpu.SemaphoreType.DMA((4, len(PIECES))),
            pltpu.SemaphoreType.DMA((4, len(PIECES))),
            pltpu.SemaphoreType.DMA((8, len(PIECES))),
            pltpu.SemaphoreType.DMA,
        ],
        compiler_params=pltpu.CompilerParams(
            collective_id=0, has_side_effects=True, vmem_limit_bytes=24 * 2**20
        ),
        name="gather",
    )(
        pltpu.with_memory_space_constraint(spectra, pltpu.HBM),
        pltpu.with_memory_space_constraint(alive_mask.reshape(1, -1), pltpu.HBM),
    )


def cross_kernel(scale, h_ref, out_ref, own, partner, ring, sems):
    me = lax.axis_index("chan")
    y, c = (me // 2) % 2, me % 2
    rows = h_ref.shape[1] * h_ref.shape[2]
    width = h_ref.shape[3]
    half = width // HALVES

    def out_copy(lag, f, piece):
        slot = lag % DEPTH
        return pltpu.make_async_copy(
            ring.at[slot, f, pl.ds(piece * half, half)],
            out_ref.at[lag, f, pl.ds(piece * half, half)],
            sems.at[slot, f, piece],
        )

    def one_lag(lag, _):
        place = 8 + c - lag
        kind = place % 2

        @pl.when(lag < 2)
        def _():
            x = h_ref[4 + y].reshape(rows, width).astype(jnp.float32)
            row = lax.broadcasted_iota(jnp.int32, x.shape, 0)
            block, group, part = (row // 8) % 2, (row // 4) % 2, (row // 2) % 2
            swapped = jnp.where(block == 0, pltpu.roll(x, rows - 8, 0), pltpu.roll(x, 8, 0))
            base = jnp.where(lag == 0, x, swapped)
            turned = jnp.where(part == 0, pltpu.roll(base, rows - 2, 0), -pltpu.roll(base, 2, 0))
            for f in range(2):
                kept = (block == kind) & (group == f)
                own[kind, f, :, pl.ds(0, width)] = jnp.where(kept, base, 0.0).astype(jnp.bfloat16)
                own[kind, f, :, pl.ds(width, width)] = jnp.where(kept, turned, 0.0).astype(jnp.bfloat16)

        @pl.when((lag == 0) | (kind == 1))
        def _():
            partner[...] = h_ref[y + place // 2].reshape(rows, width).T

        for f in range(2):
            for piece in range(HALVES):
                at = pl.ds(piece * half, half)
                product = jnp.dot(partner[at, :], own[kind, f], preferred_element_type=jnp.float32)

                @pl.when(lag >= DEPTH)
                def _():
                    out_copy(lag - DEPTH, f, piece).wait()

                ring[lag % DEPTH, f, at] = product * scale
                out_copy(lag, f, piece).start()
        return 0

    lax.fori_loop(0, LAGS, one_lag, 0)
    for lag in range(LAGS - DEPTH, LAGS):
        for f in range(2):
            for piece in range(HALVES):
                out_copy(lag, f, piece).wait()


def cross(gathered, windows):
    width = gathered.shape[3]
    return pl.pallas_call(
        functools.partial(cross_kernel, 1.0 / windows),
        out_shape=jax.ShapeDtypeStruct((LAGS, 2, width, 2 * width), jnp.float32),
        in_specs=[pl.BlockSpec(memory_space=pltpu.VMEM)],
        out_specs=pl.BlockSpec(memory_space=pltpu.HBM),
        scratch_shapes=[
            pltpu.VMEM((2, 2, 256, 2 * width), jnp.bfloat16),
            pltpu.VMEM((width, 256), jnp.bfloat16),
            pltpu.VMEM((DEPTH, 2, width, 2 * width), jnp.float32),
            pltpu.SemaphoreType.DMA((DEPTH, 2, HALVES)),
        ],
        compiler_params=pltpu.CompilerParams(vmem_limit_bytes=28 * 2**20),
        name="cross",
    )(gathered)


def plane_shards(spectra, alive_mask):
    gathered = gather(spectra, alive_mask)
    return cross(gathered, 16 * spectra.shape[2])[None]


def solution(mesh):
    def local(spectra, alive_mask):
        fits = lax.axis_size("chan") == 16 and spectra.shape == (2, 2, 2, 8192)
        return (plane_shards if fits else ring_shards)(spectra, alive_mask)

    return jax.shard_map(
        local,
        mesh=mesh,
        in_specs=(P("freq", None, "chan", None), P()),
        out_specs=P("chan", None, "freq", None, None),
        check_vma=False,
    )
```

```python
import functools

import jax
import jax.numpy as jnp
from jax import lax
from jax.experimental import pallas as pl
from jax.experimental.pallas import tpu as pltpu
from jax.sharding import PartitionSpec as P

MESH = pl.DeviceIdType.MESH
PLANES = 4
SLOTS = 16
LAGS = 9
DEPTH = 4
HALVES = 1

PIECES = [
    [(2, 3), (0, 2), (5, 1)],
    [(0, 3), (3, 3)],
    [(3, 3), (0, 3)],
    [(1, 3), (4, 2), (0, 1)],
]
MAX_PIECES = 3
NEED = 6
PASSED = {(2, 0): 3, (2, 1): 3, (1, 3): 0, (1, 2): 0}


def from_behind(block, axis, distance):
    devices = range(lax.axis_size(axis))
    route = [((i - distance) % len(devices), i) for i in devices]
    return lax.ppermute(block, axis, route)


def cross_block(own_stacked, partner_block, windows):
    product = jnp.einsum(
        "fjw,fiw->fji", partner_block, own_stacked, preferred_element_type=jnp.float32
    )
    return product / windows


def ring_shards(spectra, alive_mask):
    channel_devices = lax.axis_size("chan")
    groups = spectra.shape[0]
    block_width = spectra.shape[3] // channel_devices
    windows = spectra.shape[2] * channel_devices
    lag_count = channel_devices // 2 + 1
    real_part = spectra[:, 0]
    imag_part = spectra[:, 1]
    magnitude = jnp.sqrt(real_part * real_part + imag_part * imag_part)
    factor = alive_mask.astype(jnp.float32)[None, None, :] / jnp.maximum(magnitude, 1.0)
    whitened = (spectra * factor[:, None]).astype(jnp.bfloat16)
    regrouped = lax.all_to_all(whitened, "chan", split_axis=3, concat_axis=2, tiled=True)
    own_block = jnp.transpose(regrouped.reshape(groups, 2 * windows, block_width), (0, 2, 1))
    turned = jnp.concatenate([own_block[:, :, windows:], -own_block[:, :, :windows]], axis=2)
    own_stacked = jnp.concatenate([own_block, turned], axis=1)
    empty_band = jnp.zeros((lag_count, groups, block_width, 2 * block_width), jnp.float32)
    start_band = lax.dynamic_update_index_in_dim(
        empty_band, cross_block(own_stacked, own_block, windows), 0, 0
    )

    def four_steps(turn, carry):
        visitor, band = carry
        for repeat in range(4):
            visitor = from_behind(visitor, "chan", 1)
            band = lax.dynamic_update_index_in_dim(
                band, cross_block(own_stacked, visitor, windows), 1 + 4 * turn + repeat, 0
            )
        return (visitor, band)

    visitor, cross_band = lax.fori_loop(
        0, channel_devices // 8, four_steps, (own_block, start_band)
    )
    return cross_band[None]


def gather_kernel(x_hbm, alive_hbm, h_ref, x_buf, alive_ref, g, load_sem, recv_z, recv_y, recv_c, send_z, send_y, send_c, send_p, out_sem):
    me = lax.axis_index("chan")
    z, y, c = me // 4, (me // 2) % 2, me % 2
    y_peer = z * 4 + (1 - y) * 2 + c
    c_peer = z * 4 + y * 2 + (1 - c)
    width = x_buf.shape[1] // 16

    loads = []
    for f in range(2):
        for part in range(2):
            at = f * 2 + part
            loads.append(pltpu.make_async_copy(x_hbm.at[f, part], x_buf.at[pl.ds(2 * at, 2)], load_sem.at[at]))
    loads.append(pltpu.make_async_copy(alive_hbm, alive_ref, load_sem.at[4]))
    for load in loads:
        load.start()

    barrier = pltpu.get_barrier_semaphore()
    pl.semaphore_signal(barrier, inc=1, device_id={"chan": y_peer}, device_id_type=MESH)
    pl.semaphore_signal(barrier, inc=1, device_id={"chan": c_peer}, device_id_type=MESH)

    for hop in range(1, PLANES):
        pl.semaphore_signal(barrier, inc=1, device_id={"chan": (me + 4 * hop) % 16}, device_id_type=MESH)

    for load in loads:
        load.wait()
    for granule in range(8):
        halves = []
        for half in range(2):
            at = pl.ds((2 * granule + half) * width, width)
            x = x_buf[:, at]
            square = x * x
            row = lax.broadcasted_iota(jnp.int32, x.shape, 0)
            is_real = (row // 2) % 2 == 0
            other = jnp.where(is_real, pltpu.roll(square, 6, 0), pltpu.roll(square, 2, 0))
            magnitude = jnp.sqrt(square + other)
            factor = alive_ref[:, at].astype(jnp.float32) / jnp.maximum(magnitude, 1.0)
            halves.append(x * factor)
        tile = jnp.concatenate(halves, axis=0).astype(jnp.bfloat16)
        g[granule] = tile
        g[granule + 8] = tile

    pl.semaphore_wait(barrier, 5)

    def chip(zz, yy):
        first = lambda plane: (2 * plane + 4) % 8
        column = lambda s: s * 4 + yy * 2 + c
        others = lambda s: s * 4 + (1 - yy) * 2 + c
        sends = []

        def remote(view, src, start, length, peer, send, recv):
            return pltpu.make_async_remote_copy(
                src_ref=view, dst_ref=h_ref.at[pl.ds(start, length), src], send_sem=send, recv_sem=recv,
                device_id={"chan": peer}, device_id_type=MESH,
            )

        def go(copy):
            copy.start()
            sends.append(copy)

        def cut(k, chip_y):
            start, length = PIECES[zz][k]
            low, high = max(start, chip_y), min(start + length, chip_y + 5)
            return low, max(high - low, 0)

        def view_of(s, start, length):
            if s == zz:
                return g.at[pl.ds(first(zz) + start, length)]
            return h_ref.at[pl.ds(start, length), column(s)]

        def to_z(s, k):
            if k >= len(PIECES[s]) or (k == 0 and s in (PASSED.get((2, zz)), PASSED.get((1, zz)))):
                return
            start, length = PIECES[s][k]
            view = g.at[pl.ds(first(s) + start, length)]
            go(remote(view, me, start, length, s * 4 + yy * 2 + c, send_z.at[s, k], recv_z.at[zz, k]))

        def to_y(s, k):
            start, length = cut(k, 1 - yy)
            if not length:
                return
            go(remote(view_of(s, start, length), column(s), start, length, y_peer, send_y.at[s, k], recv_y.at[s, k]))

        def to_c(s, k, in_column):
            start, length = cut(k, yy)
            if not length:
                return
            src = column(s) if in_column else others(s)
            view = view_of(s, start, length) if in_column else h_ref.at[pl.ds(start, length), src]
            at = s if in_column else PLANES + s
            go(remote(view, src, start, length, c_peer, send_c.at[at, k], recv_c.at[at, k]))

        def from_z(s, k):
            start, length = PIECES[zz][k]
            view = g.at[pl.ds(start, length)]
            remote(view, column(s), start, length, y_peer, send_z.at[s, k], recv_z.at[s, k]).wait_recv()
            if k == 0 and (zz, s) in PASSED:
                to = PASSED[zz, s]
                view = h_ref.at[pl.ds(start, length), column(s)]
                peer = to * 4 + yy * 2 + c
                go(remote(view, column(s), PIECES[to][0][0], length, peer, send_p.at[s], recv_z.at[s, 0]))
            to_y(s, k)
            to_c(s, k, True)

        def from_y(s, k):
            start, length = cut(k, yy)
            if not length:
                return
            view = g.at[pl.ds(start, length)]
            remote(view, others(s), start, length, y_peer, send_y.at[s, k], recv_y.at[s, k]).wait_recv()
            to_c(s, k, False)

        def from_c(s, k, in_column):
            start, length = cut(k, yy)
            if not length:
                return
            src = s * 4 + (yy if in_column else 1 - yy) * 2 + (1 - c)
            at = s if in_column else PLANES + s
            view = g.at[pl.ds(start, length)]
            remote(view, src, start, length, c_peer, send_c.at[at, k], recv_c.at[at, k]).wait_recv()

        order = sorted((s for s in range(PLANES) if s != zz), key=lambda s: abs(s - zz))
        count = len(PIECES[zz])
        for k in range(count):
            to_y(zz, k)
        for s in order:
            for k in range(MAX_PIECES):
                to_z(s, k)
        for k in range(count):
            to_c(zz, k, True)
        keep = pltpu.make_async_copy(g.at[pl.ds(first(zz), NEED)], h_ref.at[:, me], out_sem)
        keep.start()
        for k in range(count):
            from_y(zz, k)
        for s in order:
            for k in range(count):
                from_z(s, k)
        for s in order:
            for k in range(count):
                from_y(s, k)
        for k in range(count):
            for in_column in (True, False):
                for s in [zz] + order:
                    from_c(s, k, in_column)
        for copy in sends:
            copy.wait_send()
        keep.wait()

    for zz in range(PLANES):
        for yy in range(2):
            pl.when((z == zz) & (y == yy))(functools.partial(chip, zz, yy))


def gather(spectra, alive_mask):
    width = spectra.shape[3] // 16
    return pl.pallas_call(
        gather_kernel,
        out_shape=jax.ShapeDtypeStruct((NEED, 16, 16, width), jnp.bfloat16),
        in_specs=[pl.BlockSpec(memory_space=pltpu.HBM)] * 2,
        out_specs=pl.BlockSpec(memory_space=pl.ANY),
        scratch_shapes=[
            pltpu.VMEM((8, 16 * width), jnp.float32),
            pltpu.VMEM((1, 16 * width), jnp.int32),
            pltpu.VMEM((SLOTS, 16, width), jnp.bfloat16),
            pltpu.SemaphoreType.DMA((5,)),
            pltpu.SemaphoreType.DMA((4, MAX_PIECES)),
            pltpu.SemaphoreType.DMA((4, MAX_PIECES)),
            pltpu.SemaphoreType.DMA((8, MAX_PIECES)),
            pltpu.SemaphoreType.DMA((4, MAX_PIECES)),
            pltpu.SemaphoreType.DMA((4, MAX_PIECES)),
            pltpu.SemaphoreType.DMA((8, MAX_PIECES)),
            pltpu.SemaphoreType.DMA((4,)),
            pltpu.SemaphoreType.DMA,
        ],
        compiler_params=pltpu.CompilerParams(
            collective_id=0, has_side_effects=True, vmem_limit_bytes=24 * 2**20
        ),
        name="gather",
    )(
        pltpu.with_memory_space_constraint(spectra, pltpu.HBM),
        pltpu.with_memory_space_constraint(alive_mask.reshape(1, -1), pltpu.HBM),
    )


def cross_kernel(scale, h_ref, out_ref, own, partner, ring, sems):
    me = lax.axis_index("chan")
    y, c = (me // 2) % 2, me % 2
    rows = h_ref.shape[1] * h_ref.shape[2]
    width = h_ref.shape[3]
    half = width // HALVES

    def out_copy(lag, f, piece):
        slot = lag % DEPTH
        return pltpu.make_async_copy(
            ring.at[slot, f, pl.ds(piece * half, half)],
            out_ref.at[lag, f, pl.ds(piece * half, half)],
            sems.at[slot, f, piece],
        )

    def one_lag(lag, _):
        place = 8 + c - lag
        kind = place % 2

        @pl.when(lag < 2)
        def _():
            x = h_ref[4 + y].reshape(rows, width).astype(jnp.float32)
            row = lax.broadcasted_iota(jnp.int32, x.shape, 0)
            block, group, part = (row // 8) % 2, (row // 4) % 2, (row // 2) % 2
            swapped = jnp.where(block == 0, pltpu.roll(x, rows - 8, 0), pltpu.roll(x, 8, 0))
            base = jnp.where(lag == 0, x, swapped)
            turned = jnp.where(part == 0, pltpu.roll(base, rows - 2, 0), -pltpu.roll(base, 2, 0))
            for f in range(2):
                kept = (block == kind) & (group == f)
                own[kind, f, :, pl.ds(0, width)] = jnp.where(kept, base, 0.0).astype(jnp.bfloat16)
                own[kind, f, :, pl.ds(width, width)] = jnp.where(kept, turned, 0.0).astype(jnp.bfloat16)

        @pl.when((lag == 0) | (kind == 1))
        def _():
            partner[...] = h_ref[y + place // 2].reshape(rows, width).T

        for f in range(2):
            for piece in range(HALVES):
                at = pl.ds(piece * half, half)
                product = jnp.dot(partner[at, :], own[kind, f], preferred_element_type=jnp.float32)

                @pl.when(lag >= DEPTH)
                def _():
                    out_copy(lag - DEPTH, f, piece).wait()

                ring[lag % DEPTH, f, at] = product * scale
                out_copy(lag, f, piece).start()
        return 0

    lax.fori_loop(0, LAGS, one_lag, 0)
    for lag in range(LAGS - DEPTH, LAGS):
        for f in range(2):
            for piece in range(HALVES):
                out_copy(lag, f, piece).wait()


def cross(gathered, windows):
    width = gathered.shape[3]
    return pl.pallas_call(
        functools.partial(cross_kernel, 1.0 / windows),
        out_shape=jax.ShapeDtypeStruct((LAGS, 2, width, 2 * width), jnp.float32),
        in_specs=[pl.BlockSpec(memory_space=pltpu.VMEM)],
        out_specs=pl.BlockSpec(memory_space=pltpu.HBM),
        scratch_shapes=[
            pltpu.VMEM((2, 2, 256, 2 * width), jnp.bfloat16),
            pltpu.VMEM((width, 256), jnp.bfloat16),
            pltpu.VMEM((DEPTH, 2, width, 2 * width), jnp.float32),
            pltpu.SemaphoreType.DMA((DEPTH, 2, HALVES)),
        ],
        compiler_params=pltpu.CompilerParams(vmem_limit_bytes=28 * 2**20),
        name="cross",
    )(gathered)


def plane_shards(spectra, alive_mask):
    gathered = gather(spectra, alive_mask)
    return cross(gathered, 16 * spectra.shape[2])[None]


def solution(mesh):
    def local(spectra, alive_mask):
        fits = lax.axis_size("chan") == 16 and spectra.shape == (2, 2, 2, 8192)
        return (plane_shards if fits else ring_shards)(spectra, alive_mask)

    return jax.shard_map(
        local,
        mesh=mesh,
        in_specs=(P("freq", None, "chan", None), P()),
        out_specs=P("chan", None, "freq", None, None),
        check_vma=False,
    )
```

```python
import functools

import jax
import jax.numpy as jnp
from jax import lax
from jax.experimental import pallas as pl
from jax.experimental.pallas import tpu as pltpu
from jax.sharding import PartitionSpec as P

MESH = pl.DeviceIdType.MESH
PLANES = 4
SLOTS = 16
LAGS = 9
DEPTH = 4
HALVES = 1

PIECES = [
    [(2, 3), (0, 2), (5, 1)],
    [(0, 3), (3, 3)],
    [(3, 3), (0, 3)],
    [(1, 3), (4, 2), (0, 1)],
]
MAX_PIECES = 3
NEED = 6
PASSED = {(2, 0): 3, (2, 1): 3, (1, 3): 0, (1, 2): 0}


def from_behind(block, axis, distance):
    devices = range(lax.axis_size(axis))
    route = [((i - distance) % len(devices), i) for i in devices]
    return lax.ppermute(block, axis, route)


def cross_block(own_stacked, partner_block, windows):
    product = jnp.einsum(
        "fjw,fiw->fji", partner_block, own_stacked, preferred_element_type=jnp.float32
    )
    return product / windows


def ring_shards(spectra, alive_mask):
    channel_devices = lax.axis_size("chan")
    groups = spectra.shape[0]
    block_width = spectra.shape[3] // channel_devices
    windows = spectra.shape[2] * channel_devices
    lag_count = channel_devices // 2 + 1
    real_part = spectra[:, 0]
    imag_part = spectra[:, 1]
    magnitude = jnp.sqrt(real_part * real_part + imag_part * imag_part)
    factor = alive_mask.astype(jnp.float32)[None, None, :] / jnp.maximum(magnitude, 1.0)
    whitened = (spectra * factor[:, None]).astype(jnp.bfloat16)
    regrouped = lax.all_to_all(whitened, "chan", split_axis=3, concat_axis=2, tiled=True)
    own_block = jnp.transpose(regrouped.reshape(groups, 2 * windows, block_width), (0, 2, 1))
    turned = jnp.concatenate([own_block[:, :, windows:], -own_block[:, :, :windows]], axis=2)
    own_stacked = jnp.concatenate([own_block, turned], axis=1)
    empty_band = jnp.zeros((lag_count, groups, block_width, 2 * block_width), jnp.float32)
    start_band = lax.dynamic_update_index_in_dim(
        empty_band, cross_block(own_stacked, own_block, windows), 0, 0
    )

    def four_steps(turn, carry):
        visitor, band = carry
        for repeat in range(4):
            visitor = from_behind(visitor, "chan", 1)
            band = lax.dynamic_update_index_in_dim(
                band, cross_block(own_stacked, visitor, windows), 1 + 4 * turn + repeat, 0
            )
        return (visitor, band)

    visitor, cross_band = lax.fori_loop(
        0, channel_devices // 8, four_steps, (own_block, start_band)
    )
    return cross_band[None]


def gather_kernel(x_hbm, alive_hbm, h_ref, x_buf, alive_ref, g, load_sem, recv_z, recv_y, recv_c, send_z, send_y, send_c, send_p, out_sem):
    me = lax.axis_index("chan")
    z, y, c = me // 4, (me // 2) % 2, me % 2
    y_peer = z * 4 + (1 - y) * 2 + c
    c_peer = z * 4 + y * 2 + (1 - c)
    width = x_buf.shape[1] // 16

    loads = []
    for f in range(2):
        for part in range(2):
            at = f * 2 + part
            loads.append(pltpu.make_async_copy(x_hbm.at[f, part], x_buf.at[pl.ds(2 * at, 2)], load_sem.at[at]))
    loads.append(pltpu.make_async_copy(alive_hbm, alive_ref, load_sem.at[4]))
    for load in loads:
        load.start()

    barrier = pltpu.get_barrier_semaphore()
    pl.semaphore_signal(barrier, inc=1, device_id={"chan": y_peer}, device_id_type=MESH)
    pl.semaphore_signal(barrier, inc=1, device_id={"chan": c_peer}, device_id_type=MESH)

    for hop in range(1, PLANES):
        pl.semaphore_signal(barrier, inc=1, device_id={"chan": (me + 4 * hop) % 16}, device_id_type=MESH)

    for load in loads:
        load.wait()
    for granule in range(8):
        halves = []
        for half in range(2):
            at = pl.ds((2 * granule + half) * width, width)
            x = x_buf[:, at]
            square = x * x
            row = lax.broadcasted_iota(jnp.int32, x.shape, 0)
            is_real = (row // 2) % 2 == 0
            other = jnp.where(is_real, pltpu.roll(square, 6, 0), pltpu.roll(square, 2, 0))
            magnitude = jnp.sqrt(square + other)
            factor = alive_ref[:, at].astype(jnp.float32) / jnp.maximum(magnitude, 1.0)
            halves.append(x * factor)
        tile = jnp.concatenate(halves, axis=0).astype(jnp.bfloat16)
        g[granule] = tile
        g[granule + 8] = tile

    pl.semaphore_wait(barrier, 5)

    def chip(zz, yy):
        first = lambda plane: (2 * plane + 4) % 8
        column = lambda s: s * 4 + yy * 2 + c
        others = lambda s: s * 4 + (1 - yy) * 2 + c
        sends = []

        def remote(view, src, start, length, peer, send, recv):
            return pltpu.make_async_remote_copy(
                src_ref=view, dst_ref=h_ref.at[pl.ds(start, length), src], send_sem=send, recv_sem=recv,
                device_id={"chan": peer}, device_id_type=MESH,
            )

        def go(copy):
            copy.start()
            sends.append(copy)

        def cut(k, chip_y):
            start, length = PIECES[zz][k]
            low, high = max(start, chip_y), min(start + length, chip_y + 5)
            return low, max(high - low, 0)

        def view_of(s, start, length):
            if s == zz:
                return g.at[pl.ds(first(zz) + start, length)]
            return h_ref.at[pl.ds(start, length), column(s)]

        def to_z(s, k):
            if k >= len(PIECES[s]) or (k == 0 and s in (PASSED.get((2, zz)), PASSED.get((1, zz)))):
                return
            start, length = PIECES[s][k]
            view = g.at[pl.ds(first(s) + start, length)]
            go(remote(view, me, start, length, s * 4 + yy * 2 + c, send_z.at[s, k], recv_z.at[zz, k]))

        def to_y(s, k):
            start, length = cut(k, 1 - yy)
            if not length:
                return
            go(remote(view_of(s, start, length), column(s), start, length, y_peer, send_y.at[s, k], recv_y.at[s, k]))

        def to_c(s, k, in_column):
            start, length = cut(k, yy)
            if not length:
                return
            src = column(s) if in_column else others(s)
            view = view_of(s, start, length) if in_column else h_ref.at[pl.ds(start, length), src]
            at = s if in_column else PLANES + s
            go(remote(view, src, start, length, c_peer, send_c.at[at, k], recv_c.at[at, k]))

        def from_z(s, k):
            start, length = PIECES[zz][k]
            view = g.at[pl.ds(start, length)]
            remote(view, column(s), start, length, y_peer, send_z.at[s, k], recv_z.at[s, k]).wait_recv()
            if k == 0 and (zz, s) in PASSED:
                to = PASSED[zz, s]
                view = h_ref.at[pl.ds(start, length), column(s)]
                peer = to * 4 + yy * 2 + c
                go(remote(view, column(s), PIECES[to][0][0], length, peer, send_p.at[s], recv_z.at[s, 0]))
            to_y(s, k)
            to_c(s, k, True)

        def from_y(s, k):
            start, length = cut(k, yy)
            if not length:
                return
            view = g.at[pl.ds(start, length)]
            remote(view, others(s), start, length, y_peer, send_y.at[s, k], recv_y.at[s, k]).wait_recv()
            to_c(s, k, False)

        def from_c(s, k, in_column):
            start, length = cut(k, yy)
            if not length:
                return
            src = s * 4 + (yy if in_column else 1 - yy) * 2 + (1 - c)
            at = s if in_column else PLANES + s
            view = g.at[pl.ds(start, length)]
            remote(view, src, start, length, c_peer, send_c.at[at, k], recv_c.at[at, k]).wait_recv()

        order = sorted((s for s in range(PLANES) if s != zz), key=lambda s: abs(s - zz))
        count = len(PIECES[zz])
        urgent = [s for s in order if (s, zz) in PASSED]
        for s in urgent:
            to_z(s, 0)
        for k in range(count):
            to_y(zz, k)
        for s in order:
            for k in range(1 if s in urgent else 0, MAX_PIECES):
                to_z(s, k)
        for k in range(count):
            to_c(zz, k, True)
        keep = pltpu.make_async_copy(g.at[pl.ds(first(zz), NEED)], h_ref.at[:, me], out_sem)
        keep.start()
        passing = [s for s in order if (zz, s) in PASSED]
        for s in passing:
            from_z(s, 0)
        for k in range(count):
            from_y(zz, k)
        for s in order:
            for k in range(1 if s in passing else 0, count):
                from_z(s, k)
        for s in order:
            for k in range(count):
                from_y(s, k)
        for k in range(count):
            for in_column in (True, False):
                for s in [zz] + order:
                    from_c(s, k, in_column)
        for copy in sends:
            copy.wait_send()
        keep.wait()

    for zz in range(PLANES):
        for yy in range(2):
            pl.when((z == zz) & (y == yy))(functools.partial(chip, zz, yy))


def gather(spectra, alive_mask):
    width = spectra.shape[3] // 16
    return pl.pallas_call(
        gather_kernel,
        out_shape=jax.ShapeDtypeStruct((NEED, 16, 16, width), jnp.bfloat16),
        in_specs=[pl.BlockSpec(memory_space=pltpu.HBM)] * 2,
        out_specs=pl.BlockSpec(memory_space=pl.ANY),
        scratch_shapes=[
            pltpu.VMEM((8, 16 * width), jnp.float32),
            pltpu.VMEM((1, 16 * width), jnp.int32),
            pltpu.VMEM((SLOTS, 16, width), jnp.bfloat16),
            pltpu.SemaphoreType.DMA((5,)),
            pltpu.SemaphoreType.DMA((4, MAX_PIECES)),
            pltpu.SemaphoreType.DMA((4, MAX_PIECES)),
            pltpu.SemaphoreType.DMA((8, MAX_PIECES)),
            pltpu.SemaphoreType.DMA((4, MAX_PIECES)),
            pltpu.SemaphoreType.DMA((4, MAX_PIECES)),
            pltpu.SemaphoreType.DMA((8, MAX_PIECES)),
            pltpu.SemaphoreType.DMA((4,)),
            pltpu.SemaphoreType.DMA,
        ],
        compiler_params=pltpu.CompilerParams(
            collective_id=0, has_side_effects=True, vmem_limit_bytes=24 * 2**20
        ),
        name="gather",
    )(
        pltpu.with_memory_space_constraint(spectra, pltpu.HBM),
        pltpu.with_memory_space_constraint(alive_mask.reshape(1, -1), pltpu.HBM),
    )


def cross_kernel(scale, h_ref, out_ref, own, partner, ring, sems):
    me = lax.axis_index("chan")
    y, c = (me // 2) % 2, me % 2
    rows = h_ref.shape[1] * h_ref.shape[2]
    width = h_ref.shape[3]
    half = width // HALVES

    def out_copy(lag, f, piece):
        slot = lag % DEPTH
        return pltpu.make_async_copy(
            ring.at[slot, f, pl.ds(piece * half, half)],
            out_ref.at[lag, f, pl.ds(piece * half, half)],
            sems.at[slot, f, piece],
        )

    def one_lag(lag, _):
        place = 8 + c - lag
        kind = place % 2

        @pl.when(lag < 2)
        def _():
            x = h_ref[4 + y].reshape(rows, width).astype(jnp.float32)
            row = lax.broadcasted_iota(jnp.int32, x.shape, 0)
            block, group, part = (row // 8) % 2, (row // 4) % 2, (row // 2) % 2
            swapped = jnp.where(block == 0, pltpu.roll(x, rows - 8, 0), pltpu.roll(x, 8, 0))
            base = jnp.where(lag == 0, x, swapped)
            turned = jnp.where(part == 0, pltpu.roll(base, rows - 2, 0), -pltpu.roll(base, 2, 0))
            for f in range(2):
                kept = (block == kind) & (group == f)
                own[kind, f, :, pl.ds(0, width)] = jnp.where(kept, base, 0.0).astype(jnp.bfloat16)
                own[kind, f, :, pl.ds(width, width)] = jnp.where(kept, turned, 0.0).astype(jnp.bfloat16)

        @pl.when((lag == 0) | (kind == 1))
        def _():
            partner[...] = h_ref[y + place // 2].reshape(rows, width).T

        for f in range(2):
            for piece in range(HALVES):
                at = pl.ds(piece * half, half)
                product = jnp.dot(partner[at, :], own[kind, f], preferred_element_type=jnp.float32)

                @pl.when(lag >= DEPTH)
                def _():
                    out_copy(lag - DEPTH, f, piece).wait()

                ring[lag % DEPTH, f, at] = product * scale
                out_copy(lag, f, piece).start()
        return 0

    lax.fori_loop(0, LAGS, one_lag, 0)
    for lag in range(LAGS - DEPTH, LAGS):
        for f in range(2):
            for piece in range(HALVES):
                out_copy(lag, f, piece).wait()


def cross(gathered, windows):
    width = gathered.shape[3]
    return pl.pallas_call(
        functools.partial(cross_kernel, 1.0 / windows),
        out_shape=jax.ShapeDtypeStruct((LAGS, 2, width, 2 * width), jnp.float32),
        in_specs=[pl.BlockSpec(memory_space=pltpu.VMEM)],
        out_specs=pl.BlockSpec(memory_space=pltpu.HBM),
        scratch_shapes=[
            pltpu.VMEM((2, 2, 256, 2 * width), jnp.bfloat16),
            pltpu.VMEM((width, 256), jnp.bfloat16),
            pltpu.VMEM((DEPTH, 2, width, 2 * width), jnp.float32),
            pltpu.SemaphoreType.DMA((DEPTH, 2, HALVES)),
        ],
        compiler_params=pltpu.CompilerParams(vmem_limit_bytes=28 * 2**20),
        name="cross",
    )(gathered)


def plane_shards(spectra, alive_mask):
    gathered = gather(spectra, alive_mask)
    return cross(gathered, 16 * spectra.shape[2])[None]


def solution(mesh):
    def local(spectra, alive_mask):
        fits = lax.axis_size("chan") == 16 and spectra.shape == (2, 2, 2, 8192)
        return (plane_shards if fits else ring_shards)(spectra, alive_mask)

    return jax.shard_map(
        local,
        mesh=mesh,
        in_specs=(P("freq", None, "chan", None), P()),
        out_specs=P("chan", None, "freq", None, None),
        check_vma=False,
    )
```
